512 devices in a mesh: seq: 64 (over y, z), head: 8 (over x, core).
Axes of the slice: x: 4, y: 8, z: 8, core: 2. Of those that a mesh axis runs over, the one named last changes fastest.
Arguments:
- queries: bfloat16 [32768, 2048], P('seq', 'head'), may hold values from -100 to 100
- keys: bfloat16 [32768, 2048], P('seq', 'head'), may hold values from -5 to 5
- values: bfloat16 [32768, 2048], P('seq', 'head'), may hold values from -6 to 6
- grad_out: bfloat16 [32768, 2048], P('seq', 'head'), may hold values from -6 to 6
- rand_blocks: int32 [256, 3], replicated, may hold values from 0 to 255, as said below
Outputs:
- context: bfloat16 [32768, 2048], P('seq', 'head')
- grad_q: bfloat16 [32768, 2048], P('seq', 'head')
- grad_k: bfloat16 [32768, 2048], P('seq', 'head')
- grad_v: bfloat16 [32768, 2048], P('seq', 'head')
The draws below stay inside these ranges and needn't reach their ends.
Inputs may be any that keep to these rules, and one draw needn't show every extreme that they name: `rand_blocks`: entry r of query block i is one of the 4 blocks of seq index (i // 4) XOR (256 // 4 // 2^(r+1)).
All inputs are finite; a program needn't handle non-finite values.
Results may differ from the reference program's by a relative error of at most 0.017.
Values may be sent and summed in bfloat16 or wider, within the bound.
No kernel may reach another device: no remote copies, remote signals or barrier semaphores. Data moves between devices by JAX's collectives and lax.ppermute only.
A program may use at most 64 MiB of HBM per device.

```python
from functools import partial
import jax
import jax.numpy as jnp
from jax import lax

DH = 128
HEADS = 16
BLK = 128
GLOBAL = 2
RAND = 3
QB_DEV = 4
QBLOCKS = 256
SEQ = 32768
N_SEQ = 64


def base_keys(key):
    shape = (QBLOCKS * BLK, HEADS * DH)
    return jnp.clip(jax.random.normal(jax.random.fold_in(key, 11), shape, jnp.float32), -5.0, 5.0)


def draw_keys(key, part):
    base = base_keys(key)
    return base.astype(jnp.bfloat16)


def draw_queries(key, part):
    key = jax.random.fold_in(key, 1)
    shape = (QBLOCKS * BLK, HEADS * DH)
    return jnp.clip(jax.random.normal(key, shape, jnp.float32), -5.0, 5.0).astype(jnp.bfloat16)


def draw_rand_blocks(key, part):
    key = jax.random.fold_in(key, 3)
    devices = QBLOCKS // QB_DEV
    owner = jnp.arange(QBLOCKS, dtype=jnp.int32) // QB_DEV
    shifts = jnp.right_shift(jnp.int32(devices), jnp.arange(RAND, dtype=jnp.int32) + 1)
    partner = jnp.bitwise_xor(owner[:, None], shifts[None, :])
    picks = jax.random.randint(key, (QBLOCKS, RAND), 0, QB_DEV, dtype=jnp.int32)
    return (partner * QB_DEV + picks).astype(jnp.int32)


def block_scale(rng, shape, split, least, largest):
    def one(dim, shards_of):
        steps = jax.random.uniform(jax.random.fold_in(jax.random.fold_in(rng, 6), dim), (shards_of,), jnp.float32, least / len(split), largest / len(split))
        return jnp.repeat(jnp.exp(steps), shape[dim] // shards_of).reshape((-1,) + (1,) * (len(shape) - dim - 1))

    factor_of = one(*split[0])
    for cut in split[1:]:
        factor_of = factor_of * one(*cut)
    return factor_of


def bell_draw(key, extent, deviation, limit, split=(), kind=jnp.bfloat16):
    values = deviation * jax.random.normal(key, extent, jnp.float32)
    if split:
        values = values * block_scale(key, extent, split, -0.22, 0.18)
    return jnp.clip(values, -limit, limit).astype(kind)


def setup_inputs(seed: int = 0) -> dict:
    streams_of = jax.random.split(jax.random.key(seed), 6)
    queries = draw_queries(jax.random.fold_in(streams_of[5], 71), 0)
    keys = draw_keys(jax.random.fold_in(streams_of[5], 71), 0)
    values = bell_draw(streams_of[2], (SEQ, HEADS * DH), 1.0, 6.0, ((0, 64), (1, 8)))
    grad_out = bell_draw(streams_of[3], (SEQ, HEADS * DH), 1.0, 6.0, ((0, 64), (1, 8)))
    rand_blocks = draw_rand_blocks(jax.random.fold_in(streams_of[5], 71), 0)
    return dict(queries=queries, keys=keys, values=values, grad_out=grad_out, rand_blocks=rand_blocks)


def rounded(x):
    return lax.optimization_barrier(x.astype(jnp.bfloat16)).astype(jnp.float32)


def block_tables(rand_blocks):
    qblock = jnp.arange(QBLOCKS, dtype=jnp.int32)
    glob = jnp.broadcast_to(jnp.arange(GLOBAL, dtype=jnp.int32)[None, :], (QBLOCKS, GLOBAL))
    window = qblock[:, None] + jnp.arange(-1, 2, dtype=jnp.int32)[None, :]
    chosen = rand_blocks.astype(jnp.int32)
    listed = jnp.concatenate([glob, window, chosen], axis=1)
    live = jnp.concatenate([jnp.ones((QBLOCKS, GLOBAL), bool), (window >= GLOBAL) & (window < QBLOCKS), chosen >= GLOBAL], axis=1)
    return jnp.clip(listed, 0, QBLOCKS - 1).astype(jnp.int32), live


def attend(q_blk, do_blk, listed_row, live_row, kblocks, vblocks):
    scale = 1.0 / (DH ** 0.5)
    query = q_blk.astype(jnp.float32).reshape(BLK, HEADS, DH)
    dout = do_blk.astype(jnp.float32).reshape(BLK, HEADS, DH)
    k_sel = kblocks[listed_row].reshape(-1, HEADS, DH).astype(jnp.float32)
    v_sel = vblocks[listed_row].reshape(-1, HEADS, DH).astype(jnp.float32)
    mask = jnp.repeat(live_row, BLK)
    scores = jnp.einsum('thd,uhd->htu', query, k_sel) * scale
    scores = jnp.where(mask[None, None, :], scores, -1e30)
    top = jnp.max(scores, axis=-1, keepdims=True)
    expo = jnp.exp(scores - top)
    probs = expo / jnp.sum(expo, axis=-1, keepdims=True)
    probs_b = rounded(probs)
    context = jnp.einsum('htu,uhd->thd', probs_b, v_sel).astype(jnp.bfloat16)
    dprobs = jnp.einsum('thd,uhd->htu', dout, v_sel)
    delta = jnp.sum(probs * dprobs, axis=-1, keepdims=True)
    dscores = rounded(probs * (dprobs - delta) * scale)
    grad_q = jnp.einsum('htu,uhd->thd', dscores, k_sel).astype(jnp.bfloat16)
    key_terms = jnp.einsum('htu,thd->uhd', dscores, query)
    value_terms = jnp.einsum('htu,thd->uhd', probs_b, dout)
    count = listed_row.shape[0]
    return (context.reshape(BLK, HEADS * DH), grad_q.reshape(BLK, HEADS * DH),
            key_terms.reshape(count, BLK, HEADS * DH), value_terms.reshape(count, BLK, HEADS * DH))


def reference(queries, keys, values, grad_out, rand_blocks):
    listed, live = block_tables(rand_blocks)
    width = HEADS * DH
    qblocks = queries.reshape(QBLOCKS, BLK, width)
    dblocks = grad_out.reshape(QBLOCKS, BLK, width)
    kblocks = keys.reshape(QBLOCKS, BLK, HEADS, DH)
    vblocks = values.reshape(QBLOCKS, BLK, HEADS, DH)
    count = listed.shape[1]
    entries = QB_DEV * count
    glob_slot = jnp.tile(jnp.arange(count, dtype=jnp.int32) < GLOBAL, QB_DEV)
    order = jnp.arange(entries, dtype=jnp.int32)

    def device_step(carry, device):
        dk_acc, dv_acc = carry
        start = device * QB_DEV
        q_dev = lax.dynamic_slice_in_dim(qblocks, start, QB_DEV, 0)
        d_dev = lax.dynamic_slice_in_dim(dblocks, start, QB_DEV, 0)
        l_dev = lax.dynamic_slice_in_dim(listed, start, QB_DEV, 0)
        v_live = lax.dynamic_slice_in_dim(live, start, QB_DEV, 0)
        ctx, dq, dk_t, dv_t = jax.vmap(partial(attend, kblocks=kblocks, vblocks=vblocks))(q_dev, d_dev, l_dev, v_live)
        ent = l_dev.reshape(-1)
        same = (ent[:, None] == ent[None, :]) & (glob_slot[:, None] == glob_slot[None, :])
        first = jnp.logical_not(jnp.any(same & (order[None, :] < order[:, None]), axis=1))
        collect = (same & first[:, None]).astype(jnp.float32)
        flag = jnp.logical_not(glob_slot) & (ent // QB_DEV != device)

        def route(tiles):
            flat = tiles.reshape(entries, BLK, width)
            summed = jnp.einsum('ef,fbw->ebw', collect, flat, precision=lax.Precision.HIGHEST)
            return jnp.where(flag[:, None, None], rounded(summed), summed)

        dk_acc = dk_acc.at[ent].add(route(dk_t))
        dv_acc = dv_acc.at[ent].add(route(dv_t))
        return (dk_acc, dv_acc), (ctx, dq)

    empty = jnp.zeros((QBLOCKS, BLK, width), jnp.float32)
    (dk_acc, dv_acc), (ctx, dq) = lax.scan(device_step, (empty, empty), jnp.arange(N_SEQ, dtype=jnp.int32))
    rows = QBLOCKS * BLK
    return (ctx.reshape(rows, width), dq.reshape(rows, width),
            dk_acc.astype(jnp.bfloat16).reshape(rows, width), dv_acc.astype(jnp.bfloat16).reshape(rows, width))
```

```python
import jax
import jax.numpy as jnp
from jax import lax
from jax.experimental import pallas as pl
from jax.experimental.pallas import tpu as pltpu
from jax.sharding import PartitionSpec as P

DH = 128
BLK = 128
GLOBAL = 2
RAND = 3
NEG = -1e30
F32 = jnp.float32
BF16 = jnp.bfloat16


def dot(a, b, ca, cb):
    return lax.dot_general(a, b, (((ca,), (cb,)), ((), ())), preferred_element_type=F32)


def attention_kernel(nblk, heads, idx_ref, bias_ref, q_ref, do_ref, k_ref, v_ref, left_ref, right_ref,
                     glob_ref, *rest):
    part_refs = rest[:RAND]
    ctx_ref, dq_ref, own_ref, gleft_ref, gright_ref, gglob_ref = rest[RAND:RAND + 6]
    gpart_refs = rest[RAND + 6:2 * RAND + 6]
    kwin, vwin, ksel, vsel, acc_win, acc_glob, acc_part = rest[2 * RAND + 6:]
    width = heads * DH
    tokens = nblk * BLK
    nwin = GLOBAL + 3
    scale = 1.0 / DH**0.5

    kwin[:BLK] = left_ref[:, :width]
    vwin[:BLK] = left_ref[:, width:]
    kwin[BLK:BLK + tokens] = k_ref[...]
    vwin[BLK:BLK + tokens] = v_ref[...]
    kwin[BLK + tokens:] = right_ref[:, :width]
    vwin[BLK + tokens:] = right_ref[:, width:]
    for h in range(heads):
        hs = slice(h * DH, (h + 1) * DH)
        ksel[:GLOBAL * BLK, hs] = glob_ref[h]
        vsel[:GLOBAL * BLK, hs] = glob_ref[heads + h]
    acc_win[...] = jnp.zeros_like(acc_win)
    acc_glob[...] = jnp.zeros_like(acc_glob)
    acc_part[...] = jnp.zeros_like(acc_part)

    def step(b, carry):
        start = pl.multiple_of(b * BLK, BLK)
        rows = pl.ds(start, BLK)
        ksel[GLOBAL * BLK:nwin * BLK] = kwin[pl.ds(start, 3 * BLK)]
        vsel[GLOBAL * BLK:nwin * BLK] = vwin[pl.ds(start, 3 * BLK)]
        picks = []
        for r in range(RAND):
            pick = idx_ref[b * RAND + r]
            picks.append(pick)
            src = pl.ds(pl.multiple_of(pick * BLK, BLK), BLK)
            dst = slice((nwin + r) * BLK, (nwin + r + 1) * BLK)
            ksel[dst] = part_refs[r][src, :width]
            vsel[dst] = part_refs[r][src, width:]
        bias = bias_ref[b]
        for h in range(heads):
            hs = slice(h * DH, (h + 1) * DH)
            query = q_ref[rows, hs]
            dout = do_ref[rows, hs]
            keys = ksel[:, hs]
            vals = vsel[:, hs]
            scores = dot(query, keys, 1, 1) * scale + bias
            dprobs = dot(dout, vals, 1, 1)
            top = jnp.max(scores, axis=-1, keepdims=True)
            expo = jnp.exp(scores - top)
            probs = expo * (1.0 / jnp.sum(expo, axis=-1, keepdims=True))
            probs_b = probs.astype(BF16)
            delta = jnp.sum(probs * dprobs, axis=-1, keepdims=True)
            dscores = (probs * (dprobs - delta) * scale).astype(BF16)
            ctx_ref[rows, hs] = dot(probs_b, vals, 1, 0).astype(BF16)
            dq_ref[rows, hs] = dot(dscores, keys, 1, 0).astype(BF16)
            kterm = dot(query.T, dscores, 1, 0)
            vterm = dot(dout.T, probs_b, 1, 0)
            for base, term in ((h * DH, kterm), (width + h * DH, vterm)):
                at = slice(base, base + DH)
                for g in range(GLOBAL):
                    acc_glob[g, at] += term[:, g * BLK:(g + 1) * BLK]
                for w in range(3):
                    o = GLOBAL + w
                    acc_win[b + w, at] += term[:, o * BLK:(o + 1) * BLK]
                for r in range(RAND):
                    o = nwin + r
                    acc_part[r, picks[r], at] += term[:, o * BLK:(o + 1) * BLK]
        return carry

    lax.fori_loop(0, nblk, step, 0)
    gleft_ref[...] = acc_win[0].astype(BF16)
    gright_ref[...] = acc_win[nblk + 1].astype(BF16)
    own_ref[...] = acc_win[1:nblk + 1]
    gglob_ref[...] = acc_glob[...].astype(BF16)
    for r in range(RAND):
        gpart_refs[r][...] = acc_part[r].astype(BF16)


def finish_kernel(nblk, heads, first_ref, own_ref, low_ref, high_ref, glob_ref, *rest):
    part_refs = rest[:RAND]
    gk_ref, gv_ref = rest[RAND:]
    first = first_ref[0].astype(F32)
    width = heads * DH
    for b in range(nblk):
        rows = slice(b * BLK, (b + 1) * BLK)
        for c in range(2 * heads):
            at = slice(c * DH, (c + 1) * DH)
            total = own_ref[b, at]
            for r in range(RAND):
                total = total + part_refs[r][b, at].astype(F32)
            if b == 0:
                total = total + low_ref[at].astype(F32)
            if b == nblk - 1:
                total = total + high_ref[at].astype(F32)
            if b < GLOBAL:
                total = jnp.where(first > 0, glob_ref[b, at].astype(F32), total)
            out = gk_ref if c < heads else gv_ref
            h = c % heads
            out[rows, h * DH:(h + 1) * DH] = total.T.astype(BF16)


def shards(queries, keys, values, grad_out, rand_blocks):
    n_seq = lax.axis_size("seq")
    myself = lax.axis_index("seq")
    tokens, width = queries.shape
    nblk = tokens // BLK
    heads = width // DH
    nwin = GLOBAL + 3
    up = [(i, i + 1) for i in range(n_seq - 1)]
    down = [(j, i) for i, j in up]
    masks = [n_seq >> (r + 1) for r in range(RAND)]

    def partner(x, r):
        return lax.ppermute(x, "seq", [(i, i ^ masks[r]) for i in range(n_seq)])

    kv = jnp.concatenate([keys, values], axis=1)
    fetched = [partner(kv, r) for r in range(RAND)]
    left = lax.ppermute(kv[tokens - BLK:], "seq", up)
    right = lax.ppermute(kv[:BLK], "seq", down)

    cols = 2 * heads
    grows = GLOBAL * BLK
    unit = cols * grows // n_seq
    glob = kv[:grows].reshape(grows, cols, DH).transpose(1, 0, 2).reshape(n_seq, unit, DH)
    piece = lax.all_to_all(glob, "seq", 0, 0, tiled=True)[0]
    glob = lax.all_to_all(jnp.broadcast_to(piece[None], (n_seq, unit, DH)), "seq", 0, 0, tiled=True)
    glob = glob.reshape(cols, grows, DH)

    mine = lax.dynamic_slice_in_dim(rand_blocks, myself * nblk, nblk, 0)
    picks = (mine % nblk).reshape(-1)
    qblock = myself * nblk + jnp.arange(nblk, dtype=jnp.int32)
    window = qblock[:, None] + jnp.arange(-1, 2, dtype=jnp.int32)[None, :]
    live = jnp.concatenate(
        [jnp.ones((nblk, GLOBAL), bool), (window >= GLOBAL) & (window < nblk * n_seq), mine >= GLOBAL], axis=1)
    bias = jnp.repeat(jnp.where(live, 0.0, NEG).astype(F32), BLK, axis=1)[:, None, :]

    smem = pl.BlockSpec(memory_space=pltpu.SMEM)
    vmem = pl.BlockSpec(memory_space=pltpu.VMEM)
    sds = jax.ShapeDtypeStruct
    nkeys = (nwin + RAND) * BLK
    outs = pl.pallas_call(
        lambda *refs: attention_kernel(nblk, heads, *refs),
        out_shape=[
            sds((tokens, width), BF16), sds((tokens, width), BF16),
            sds((nblk, 2 * width, BLK), F32), sds((2 * width, BLK), BF16), sds((2 * width, BLK), BF16),
            sds((GLOBAL, 2 * width, BLK), BF16),
        ] + [sds((nblk, 2 * width, BLK), BF16)] * RAND,
        in_specs=[smem] + [vmem] * (8 + RAND),
        out_specs=[vmem] * (6 + RAND),
        scratch_shapes=[
            pltpu.VMEM((tokens + 2 * BLK, width), BF16), pltpu.VMEM((tokens + 2 * BLK, width), BF16),
            pltpu.VMEM((nkeys, width), BF16), pltpu.VMEM((nkeys, width), BF16),
            pltpu.VMEM((nblk + 2, 2 * width, BLK), F32), pltpu.VMEM((GLOBAL, 2 * width, BLK), F32),
            pltpu.VMEM((RAND, nblk, 2 * width, BLK), F32),
        ],
        compiler_params=pltpu.CompilerParams(vmem_limit_bytes=48 * 1024 * 1024),
        name="attention",
    )(picks, bias, queries, grad_out, keys, values, left, right, glob, *fetched)
    context, grad_q, own, gleft, gright, gglob = outs[:6]
    gparts = outs[6:]

    back = [partner(gparts[r], r) for r in range(RAND)]
    high = lax.ppermute(gleft, "seq", down)
    low = lax.ppermute(gright, "seq", up)
    terms = lax.all_to_all(gglob.reshape(n_seq, unit, DH), "seq", 0, 0, tiled=True)
    summed = jnp.sum(terms.astype(F32), axis=0).astype(BF16)
    gsum = lax.all_to_all(jnp.broadcast_to(summed[None], (n_seq, unit, DH)), "seq", 0, 0, tiled=True)
    gsum = gsum.reshape(GLOBAL, 2 * width, BLK)
    first = (myself == 0).astype(jnp.int32).reshape(1)

    grad_k, grad_v = pl.pallas_call(
        lambda *refs: finish_kernel(nblk, heads, *refs),
        out_shape=[sds((tokens, width), BF16), sds((tokens, width), BF16)],
        in_specs=[smem] + [vmem] * (4 + RAND),
        out_specs=[vmem] * 2,
        compiler_params=pltpu.CompilerParams(vmem_limit_bytes=48 * 1024 * 1024),
        name="finish",
    )(first, own, low, high, gsum, *back)
    return context, grad_q, grad_k, grad_v


def solution(mesh):
    specs = (P("seq", "head"),) * 4
    return jax.shard_map(shards, mesh=mesh, in_specs=specs + (P(),), out_specs=specs, check_vma=False)
```

```python
import jax
import jax.numpy as jnp
from jax import lax
from jax.experimental import pallas as pl
from jax.experimental.pallas import tpu as pltpu
from jax.sharding import Mesh, PartitionSpec as P

DH = 128
BLK = 128
GLOBAL = 2
RAND = 3
NEG = -1e30
F32 = jnp.float32
BF16 = jnp.bfloat16
SEQ_AXES = ("y", "z")
VMEM_LIMIT = 48 * 1024 * 1024


def dot(a, b, ca, cb):
    return lax.dot_general(a, b, (((ca,), (cb,)), ((), ())), preferred_element_type=F32)


def attention_kernel(nblk, heads, slot_ref, idx_ref, bias_ref, q_ref, do_ref, k_ref, v_ref, left_ref,
                     right_ref, glob_ref, *rest):
    part_refs = rest[:RAND]
    ctx_ref, dq_ref, own_ref, gleft_ref, gright_ref, gglob_ref, stat_ref = rest[RAND:RAND + 7]
    kwin, vwin, ksel, vsel, acc_win, acc_glob = rest[RAND + 7:]
    width = heads * DH
    tokens = nblk * BLK
    nwin = GLOBAL + 3
    scale = 1.0 / DH**0.5

    kwin[:BLK] = left_ref[:, :width]
    vwin[:BLK] = left_ref[:, width:]
    kwin[BLK:BLK + tokens] = k_ref[...]
    vwin[BLK:BLK + tokens] = v_ref[...]
    kwin[BLK + tokens:] = right_ref[:, :width]
    vwin[BLK + tokens:] = right_ref[:, width:]
    for h in range(heads):
        hs = slice(h * DH, (h + 1) * DH)
        ksel[:GLOBAL * BLK, hs] = glob_ref[h]
        vsel[:GLOBAL * BLK, hs] = glob_ref[heads + h]
    acc_win[...] = jnp.zeros_like(acc_win)
    acc_glob[...] = jnp.zeros_like(acc_glob)
    lane = lax.broadcasted_iota(jnp.int32, (BLK, BLK), 1)

    def step(b, carry):
        start = pl.multiple_of(b * BLK, BLK)
        rows = pl.ds(start, BLK)
        ksel[GLOBAL * BLK:nwin * BLK] = kwin[pl.ds(start, 3 * BLK)]
        vsel[GLOBAL * BLK:nwin * BLK] = vwin[pl.ds(start, 3 * BLK)]
        for r in range(RAND):
            src = pl.ds(pl.multiple_of(idx_ref[b * RAND + r] * BLK, BLK), BLK)
            dst = slice((nwin + r) * BLK, (nwin + r + 1) * BLK)
            ksel[dst] = part_refs[r][0, src, :width]
            vsel[dst] = part_refs[r][0, src, width:]
        bias = bias_ref[b]
        stats = jnp.zeros((BLK, BLK), F32)
        for h in range(heads):
            hs = slice(h * DH, (h + 1) * DH)
            query = q_ref[rows, hs]
            dout = do_ref[rows, hs]
            keys = ksel[:, hs]
            vals = vsel[:, hs]
            scores = dot(query, keys, 1, 1) * scale + bias
            dprobs = dot(dout, vals, 1, 1)
            top = jnp.max(scores, axis=-1, keepdims=True)
            expo = jnp.exp(scores - top)
            inv = 1.0 / jnp.sum(expo, axis=-1, keepdims=True)
            probs = expo * inv
            probs_b = probs.astype(BF16)
            delta = jnp.sum(probs * dprobs, axis=-1, keepdims=True)
            dscores = (probs * (dprobs - delta) * scale).astype(BF16)
            ctx_ref[rows, hs] = dot(probs_b, vals, 1, 0).astype(BF16)
            dq_ref[rows, hs] = dot(dscores, keys, 1, 0).astype(BF16)
            kterm = dot(query.T, dscores[:, :nwin * BLK], 1, 0)
            vterm = dot(dout.T, probs_b[:, :nwin * BLK], 1, 0)
            for base, term in ((h * DH, kterm), (width + h * DH, vterm)):
                at = slice(base, base + DH)
                for g in range(GLOBAL):
                    acc_glob[g, at] += term[:, g * BLK:(g + 1) * BLK]
                for w in range(3):
                    o = GLOBAL + w
                    acc_win[b + w, at] += term[:, o * BLK:(o + 1) * BLK]
            for n, stat in enumerate((top, inv, delta)):
                stats = jnp.where(lane == 3 * h + n, stat, stats)
        stat_ref[:, rows] = stats.T[:8]
        return carry

    lax.fori_loop(0, nblk, step, 0)
    gleft_ref[...] = acc_win[0].astype(BF16)
    gright_ref[...] = acc_win[nblk + 1].astype(BF16)
    own_ref[...] = acc_win[1:nblk + 1]
    gglob_ref[...] = acc_glob[...].astype(BF16)


def owner_kernel(nblk, heads, slot_ref, idx_ref, live_ref, k_ref, v_ref, *rest):
    stat_refs = rest[:RAND]
    part_refs = rest[RAND:2 * RAND]
    acc_ref, = rest[2 * RAND:]
    width = heads * DH
    scale = 1.0 / DH**0.5
    acc_ref[...] = jnp.zeros_like(acc_ref)

    def step(b, carry):
        rows = pl.ds(pl.multiple_of(b * BLK, BLK), BLK)
        for r in range(RAND):
            home = pl.ds(pl.multiple_of(idx_ref[b * RAND + r] * BLK, BLK), BLK)
            bias = jnp.where(live_ref[b * RAND + r] > 0, 0.0, NEG)
            for h in range(heads):
                hs = slice(h * DH, (h + 1) * DH)
                vs = slice(width + h * DH, width + (h + 1) * DH)
                query = part_refs[r][0, rows, hs]
                dout = part_refs[r][0, rows, vs]
                top, inv, delta = (stat_refs[r][3 * h + n:3 * h + n + 1, rows] for n in range(3))
                scores = dot(k_ref[home, hs], query, 1, 1) * scale + bias
                probs = jnp.exp(scores - top) * inv
                dprobs = dot(v_ref[home, hs], dout, 1, 1)
                dscores = (probs * (dprobs - delta) * scale).astype(BF16)
                acc_ref[home, hs] += dot(dscores, query, 1, 0)
                acc_ref[home, vs] += dot(probs.astype(BF16), dout, 1, 0)
        return carry

    lax.fori_loop(0, nblk, step, 0)


def finish_kernel(nblk, heads, first_ref, own_ref, part_ref, low_ref, high_ref, glob_ref, gk_ref, gv_ref):
    first = first_ref[0].astype(F32)
    for b in range(nblk):
        rows = slice(b * BLK, (b + 1) * BLK)
        for c in range(2 * heads):
            at = slice(c * DH, (c + 1) * DH)
            total = own_ref[b, at]
            if b == 0:
                total = total + low_ref[at].astype(F32)
            if b == nblk - 1:
                total = total + high_ref[at].astype(F32)
            if b < GLOBAL:
                total = jnp.where(first > 0, glob_ref[b, at].astype(F32), total)
            out = gk_ref if c < heads else gv_ref
            h = c % heads
            out[rows, h * DH:(h + 1) * DH] = (total.T + part_ref[rows, at]).astype(BF16)


def whole(shape):
    return pl.BlockSpec(shape, lambda i, *s: (0,) * len(shape))


def slot(shape, r):
    return pl.BlockSpec((1,) + shape, lambda i, s, *t: (s[r], 0, 0))


def exchange(x, axis):
    return lax.all_to_all(x, axis, 0, 0, tiled=True)


def spread(piece, count):
    return jnp.broadcast_to(piece[None], (count,) + piece.shape)


def total(pieces):
    return jnp.sum(pieces.astype(F32), axis=0).astype(BF16)


def shards(queries, keys, values, grad_out, rand_blocks):
    ny, nz = lax.axis_size("y"), lax.axis_size("z")
    n_seq = ny * nz
    at_y, at_z = lax.axis_index("y"), lax.axis_index("z")
    myself = at_y * nz + at_z
    tokens, width = queries.shape
    nblk = tokens // BLK
    heads = width // DH
    nwin = GLOBAL + 3
    nkeys = (nwin + RAND) * BLK
    up = [(i, i + 1) for i in range(n_seq - 1)]
    down = [(j, i) for i, j in up]
    masks = [ny >> (r + 1) for r in range(RAND)]
    sds = jax.ShapeDtypeStruct
    params = pltpu.CompilerParams(vmem_limit_bytes=VMEM_LIMIT)

    kv = jnp.concatenate([keys, values], axis=1)
    qd = jnp.concatenate([queries, grad_out], axis=1)
    all_kv = lax.all_gather(kv, "y")
    left = lax.ppermute(kv[tokens - BLK:], SEQ_AXES, up)
    right = lax.ppermute(kv[:BLK], SEQ_AXES, down)

    cols = 2 * heads
    grows = GLOBAL * BLK
    glob = kv[:grows].reshape(grows, cols, DH).transpose(1, 0, 2).reshape(nz, -1, DH)
    piece = exchange(glob, "z")[0]
    piece = exchange(spread(piece, ny), "y")[0]
    glob = exchange(spread(piece, nz), "z").reshape(cols, grows, DH)

    slots = jnp.stack([at_y ^ m for m in masks]).astype(jnp.int32)
    mine = lax.dynamic_slice_in_dim(rand_blocks, myself * nblk, nblk, 0)
    picks = (mine % nblk).reshape(-1)
    qblock = myself * nblk + jnp.arange(nblk, dtype=jnp.int32)
    window = qblock[:, None] + jnp.arange(-1, 2, dtype=jnp.int32)[None, :]
    live = jnp.concatenate(
        [jnp.ones((nblk, GLOBAL), bool), (window >= GLOBAL) & (window < nblk * n_seq), mine >= GLOBAL], axis=1)
    bias = jnp.repeat(jnp.where(live, 0.0, NEG).astype(F32), BLK, axis=1)[:, None, :]
    theirs = jnp.stack(
        [lax.dynamic_slice(rand_blocks, (((at_y ^ m) * nz + at_z) * nblk, r), (nblk, 1))[:, 0]
         for r, m in enumerate(masks)], axis=1)
    homes = (theirs % nblk).reshape(-1)
    alive = (theirs >= GLOBAL).astype(jnp.int32).reshape(-1)

    tw = (tokens, width)
    pair = (tokens, 2 * width)
    context, grad_q, own, gleft, gright, gglob, stats = pl.pallas_call(
        lambda *refs: attention_kernel(nblk, heads, *refs),
        out_shape=[
            sds(tw, BF16), sds(tw, BF16), sds((nblk, 2 * width, BLK), F32), sds((2 * width, BLK), BF16),
            sds((2 * width, BLK), BF16), sds((GLOBAL, 2 * width, BLK), BF16), sds((8, tokens), F32),
        ],
        grid_spec=pltpu.PrefetchScalarGridSpec(
            num_scalar_prefetch=2,
            grid=(1,),
            in_specs=[whole((nblk, 1, nkeys))] + [whole(tw)] * 4 + [whole((BLK, 2 * width))] * 2
            + [whole((cols, grows, DH))] + [slot(pair, r) for r in range(RAND)],
            out_specs=[whole(tw), whole(tw), whole((nblk, 2 * width, BLK)), whole((2 * width, BLK)),
                       whole((2 * width, BLK)), whole((GLOBAL, 2 * width, BLK)), whole((8, tokens))],
            scratch_shapes=[
                pltpu.VMEM((tokens + 2 * BLK, width), BF16), pltpu.VMEM((tokens + 2 * BLK, width), BF16),
                pltpu.VMEM((nkeys, width), BF16), pltpu.VMEM((nkeys, width), BF16),
                pltpu.VMEM((nblk + 2, 2 * width, BLK), F32), pltpu.VMEM((GLOBAL, 2 * width, BLK), F32),
            ],
        ),
        compiler_params=params,
        name="attention",
    )(slots, picks, bias, queries, grad_out, keys, values, left, right, glob, *([all_kv] * RAND))

    all_qd = lax.all_gather(qd, "y")
    pieces = total(exchange(gglob.reshape(nz, -1, DH), "z"))
    high = lax.ppermute(gleft, SEQ_AXES, down)
    low = lax.ppermute(gright, SEQ_AXES, up)
    their_stats = [lax.ppermute(stats, "y", [(i, i ^ m) for i in range(ny)]) for m in masks]
    pieces = total(exchange(spread(pieces, ny), "y"))
    gsum = exchange(spread(pieces, nz), "z").reshape(GLOBAL, 2 * width, BLK)

    part = pl.pallas_call(
        lambda *refs: owner_kernel(nblk, heads, *refs),
        out_shape=sds(pair, F32),
        grid_spec=pltpu.PrefetchScalarGridSpec(
            num_scalar_prefetch=3,
            grid=(1,),
            in_specs=[whole(tw)] * 2 + [whole((8, tokens))] * RAND + [slot(pair, r) for r in range(RAND)],
            out_specs=whole(pair),
        ),
        compiler_params=params,
        name="owner",
    )(slots, homes, alive, keys, values, *their_stats, *([all_qd] * RAND))

    first = (myself == 0).astype(jnp.int32).reshape(1)
    smem = pl.BlockSpec(memory_space=pltpu.SMEM)
    vmem = pl.BlockSpec(memory_space=pltpu.VMEM)
    grad_k, grad_v = pl.pallas_call(
        lambda *refs: finish_kernel(nblk, heads, *refs),
        out_shape=[sds(tw, BF16), sds(tw, BF16)],
        in_specs=[smem] + [vmem] * 5,
        out_specs=[vmem] * 2,
        compiler_params=params,
        name="finish",
    )(first, own, part, low, high, gsum)
    return context, grad_q, grad_k, grad_v


def solution(mesh):
    grid = Mesh(mesh.devices.reshape(8, 8, 8), ("y", "z", "head"))
    specs = (P(SEQ_AXES, "head"),) * 4
    return jax.shard_map(shards, mesh=grid, in_specs=specs + (P(),), out_specs=specs, check_vma=False)
```

```python
import jax
import jax.numpy as jnp
from jax import lax
from jax.experimental import pallas as pl
from jax.experimental.pallas import tpu as pltpu
from jax.sharding import Mesh, PartitionSpec as P

DH = 128
BLK = 128
GLOBAL = 2
RAND = 3
NEG = -1e30
F32 = jnp.float32
BF16 = jnp.bfloat16
SEQ_AXES = ("y", "z")
VMEM_LIMIT = 48 * 1024 * 1024


def dot(a, b, ca, cb):
    return lax.dot_general(a, b, (((ca,), (cb,)), ((), ())), preferred_element_type=F32)


def attention_kernel(nblk, heads, idx_ref, bias_ref, q_ref, do_ref, k_ref, v_ref, left_ref, right_ref,
                     glob_ref, *rest):
    part_refs = rest[:RAND]
    ctx_ref, dq_ref, own_ref, gleft_ref, gright_ref, gglob_ref = rest[RAND:RAND + 6]
    gpart_refs = rest[RAND + 6:2 * RAND + 6]
    kwin, vwin, ksel, vsel, acc_win, acc_glob, acc_part = rest[2 * RAND + 6:]
    width = heads * DH
    tokens = nblk * BLK
    nwin = GLOBAL + 3
    scale = 1.0 / DH**0.5

    kwin[:BLK] = left_ref[:, :width]
    vwin[:BLK] = left_ref[:, width:]
    kwin[BLK:BLK + tokens] = k_ref[...]
    vwin[BLK:BLK + tokens] = v_ref[...]
    kwin[BLK + tokens:] = right_ref[:, :width]
    vwin[BLK + tokens:] = right_ref[:, width:]
    ksel[:GLOBAL * BLK] = glob_ref[:, :width]
    vsel[:GLOBAL * BLK] = glob_ref[:, width:]
    acc_win[...] = jnp.zeros_like(acc_win)
    acc_glob[...] = jnp.zeros_like(acc_glob)
    acc_part[...] = jnp.zeros_like(acc_part)

    def step(b, carry):
        start = pl.multiple_of(b * BLK, BLK)
        rows = pl.ds(start, BLK)
        ksel[GLOBAL * BLK:nwin * BLK] = kwin[pl.ds(start, 3 * BLK)]
        vsel[GLOBAL * BLK:nwin * BLK] = vwin[pl.ds(start, 3 * BLK)]
        picks = []
        for r in range(RAND):
            pick = idx_ref[b * RAND + r]
            picks.append(pick)
            src = pl.ds(pl.multiple_of(pick * BLK, BLK), BLK)
            dst = slice((nwin + r) * BLK, (nwin + r + 1) * BLK)
            ksel[dst] = part_refs[r][src, :width]
            vsel[dst] = part_refs[r][src, width:]
        bias = bias_ref[b]
        for h in range(heads):
            hs = slice(h * DH, (h + 1) * DH)
            query = q_ref[rows, hs]
            dout = do_ref[rows, hs]
            keys = ksel[:, hs]
            vals = vsel[:, hs]
            scores = dot(query, keys, 1, 1) * scale + bias
            dprobs = dot(dout, vals, 1, 1)
            top = jnp.max(scores, axis=-1, keepdims=True)
            expo = jnp.exp(scores - top)
            probs = expo * (1.0 / jnp.sum(expo, axis=-1, keepdims=True))
            probs_b = probs.astype(BF16)
            delta = jnp.sum(probs * dprobs, axis=-1, keepdims=True)
            dscores = (probs * (dprobs - delta) * scale).astype(BF16)
            ctx_ref[rows, hs] = dot(probs_b, vals, 1, 0).astype(BF16)
            dq_ref[rows, hs] = dot(dscores, keys, 1, 0).astype(BF16)
            kterm = dot(query.T, dscores, 1, 0)
            vterm = dot(dout.T, probs_b, 1, 0)
            for base, term in ((h * DH, kterm), (width + h * DH, vterm)):
                at = slice(base, base + DH)
                for g in range(GLOBAL):
                    acc_glob[g, at] += term[:, g * BLK:(g + 1) * BLK]
                for w in range(3):
                    o = GLOBAL + w
                    acc_win[b + w, at] += term[:, o * BLK:(o + 1) * BLK]
                for r in range(RAND):
                    o = nwin + r
                    acc_part[r, picks[r], at] += term[:, o * BLK:(o + 1) * BLK]
        return carry

    lax.fori_loop(0, nblk, step, 0)
    gleft_ref[...] = acc_win[0].astype(BF16)
    gright_ref[...] = acc_win[nblk + 1].astype(BF16)
    own_ref[...] = acc_win[1:nblk + 1]
    gglob_ref[...] = acc_glob[...].astype(BF16)
    for r in range(RAND):
        gpart_refs[r][...] = acc_part[r].astype(BF16)


def finish_kernel(nblk, heads, first_ref, own_ref, low_ref, high_ref, glob_ref, *rest):
    part_refs = rest[:RAND]
    gk_ref, gv_ref = rest[RAND:]
    first = first_ref[0].astype(F32)
    width = heads * DH
    for b in range(nblk):
        rows = slice(b * BLK, (b + 1) * BLK)
        for c in range(2 * heads):
            at = slice(c * DH, (c + 1) * DH)
            total = own_ref[b, at]
            for r in range(RAND):
                total = total + part_refs[r][b, at].astype(F32)
            if b == 0:
                total = total + low_ref[at].astype(F32)
            if b == nblk - 1:
                total = total + high_ref[at].astype(F32)
            if b < GLOBAL:
                total = jnp.where(first > 0, glob_ref[b, at].astype(F32), total)
            out = gk_ref if c < heads else gv_ref
            h = c % heads
            out[rows, h * DH:(h + 1) * DH] = total.T.astype(BF16)


def exchange(x, axis):
    return lax.all_to_all(x, axis, 0, 0, tiled=True)


def spread(piece, count):
    return jnp.broadcast_to(piece[None], (count,) + piece.shape)


def total(pieces):
    return jnp.sum(pieces.astype(F32), axis=0).astype(BF16)


def tie(*values):
    return lax.optimization_barrier(values)


def shards(queries, keys, values, grad_out, rand_blocks):
    ny, nz = lax.axis_size("y"), lax.axis_size("z")
    n_seq = ny * nz
    myself = lax.axis_index("y") * nz + lax.axis_index("z")
    tokens, width = queries.shape
    nblk = tokens // BLK
    heads = width // DH
    nwin = GLOBAL + 3
    nkeys = (nwin + RAND) * BLK
    up = [(i, i + 1) for i in range(n_seq - 1)]
    down = [(j, i) for i, j in up]
    masks = [ny >> (r + 1) for r in range(RAND)]
    sds = jax.ShapeDtypeStruct
    params = pltpu.CompilerParams(vmem_limit_bytes=VMEM_LIMIT)

    def partner(x, r):
        return lax.ppermute(x, "y", [(i, i ^ masks[r]) for i in range(ny)])

    grows = GLOBAL * BLK
    glob = jnp.concatenate([keys[:grows], values[:grows]], axis=1)
    piece = exchange(glob.reshape(nz, grows // nz, 2 * width), "z")[0]
    kv = jnp.concatenate([keys, values], axis=1)
    left = lax.ppermute(kv[tokens - BLK:], SEQ_AXES, up)
    right = lax.ppermute(kv[:BLK], SEQ_AXES, down)
    far = partner(kv, 0)
    kv, piece = tie(kv, piece)
    fetched = [far] + [partner(kv, r) for r in range(1, RAND)]
    piece = exchange(spread(piece, ny), "y")[0]
    glob = exchange(spread(piece, nz), "z").reshape(grows, 2 * width)

    mine = lax.dynamic_slice_in_dim(rand_blocks, myself * nblk, nblk, 0)
    picks = (mine % nblk).reshape(-1)
    qblock = myself * nblk + jnp.arange(nblk, dtype=jnp.int32)
    window = qblock[:, None] + jnp.arange(-1, 2, dtype=jnp.int32)[None, :]
    live = jnp.concatenate(
        [jnp.ones((nblk, GLOBAL), bool), (window >= GLOBAL) & (window < nblk * n_seq), mine >= GLOBAL], axis=1)
    bias = jnp.repeat(jnp.where(live, 0.0, NEG).astype(F32), BLK, axis=1)[:, None, :]

    smem = pl.BlockSpec(memory_space=pltpu.SMEM)
    vmem = pl.BlockSpec(memory_space=pltpu.VMEM)
    outs = pl.pallas_call(
        lambda *refs: attention_kernel(nblk, heads, *refs),
        out_shape=[
            sds((tokens, width), BF16), sds((tokens, width), BF16),
            sds((nblk, 2 * width, BLK), F32), sds((2 * width, BLK), BF16), sds((2 * width, BLK), BF16),
            sds((GLOBAL, 2 * width, BLK), BF16),
        ] + [sds((nblk, 2 * width, BLK), BF16)] * RAND,
        in_specs=[smem] + [vmem] * (8 + RAND),
        out_specs=[vmem] * (6 + RAND),
        scratch_shapes=[
            pltpu.VMEM((tokens + 2 * BLK, width), BF16), pltpu.VMEM((tokens + 2 * BLK, width), BF16),
            pltpu.VMEM((nkeys, width), BF16), pltpu.VMEM((nkeys, width), BF16),
            pltpu.VMEM((nblk + 2, 2 * width, BLK), F32), pltpu.VMEM((GLOBAL, 2 * width, BLK), F32),
            pltpu.VMEM((RAND, nblk, 2 * width, BLK), F32),
        ],
        compiler_params=params,
        name="attention",
    )(picks, bias, queries, grad_out, keys, values, left, right, glob, *fetched)
    context, grad_q, own, gleft, gright, gglob = outs[:6]
    gparts = outs[6:]

    pieces = total(exchange(gglob.reshape(nz, -1, DH), "z"))
    far = partner(gparts[0], 0)
    far, gleft, gright, *gnear = tie(far, gleft, gright, *gparts[1:])
    back = [far] + [partner(g, r + 1) for r, g in enumerate(gnear)]
    high = lax.ppermute(gleft, SEQ_AXES, down)
    low = lax.ppermute(gright, SEQ_AXES, up)
    pieces = total(exchange(spread(pieces, ny), "y"))
    gsum = exchange(spread(pieces, nz), "z").reshape(GLOBAL, 2 * width, BLK)

    first = (myself == 0).astype(jnp.int32).reshape(1)
    grad_k, grad_v = pl.pallas_call(
        lambda *refs: finish_kernel(nblk, heads, *refs),
        out_shape=[sds((tokens, width), BF16), sds((tokens, width), BF16)],
        in_specs=[smem] + [vmem] * (4 + RAND),
        out_specs=[vmem] * 2,
        compiler_params=params,
        name="finish",
    )(first, own, low, high, gsum, *back)
    return context, grad_q, grad_k, grad_v


def solution(mesh):
    grid = Mesh(mesh.devices.reshape(8, 8, 8), ("y", "z", "head"))
    specs = (P(SEQ_AXES, "head"),) * 4
    return jax.shard_map(shards, mesh=grid, in_specs=specs + (P(),), out_specs=specs, check_vma=False)
```

```python
import jax
import jax.numpy as jnp
from jax import lax
from jax.experimental import pallas as pl
from jax.experimental.pallas import tpu as pltpu
from jax.sharding import Mesh, PartitionSpec as P

DH = 128
BLK = 128
GLOBAL = 2
RAND = 3
NEG = -1e30
F32 = jnp.float32
BF16 = jnp.bfloat16
SEQ_AXES = ("y", "z")
VMEM_LIMIT = 48 * 1024 * 1024


def dot(a, b, ca, cb):
    return lax.dot_general(a, b, (((ca,), (cb,)), ((), ())), preferred_element_type=F32)


def attention_kernel(nblk, heads, idx_ref, bias_ref, q_ref, do_ref, k_ref, v_ref, left_ref, right_ref,
                     glob_ref, *rest):
    part_refs = rest[:RAND]
    ctx_ref, dq_ref, own_ref, gleft_ref, gright_ref, gglob_ref = rest[RAND:RAND + 6]
    gpart_refs = rest[RAND + 6:2 * RAND + 6]
    kwin, vwin, ksel, vsel, acc_win, acc_glob, acc_part = rest[2 * RAND + 6:]
    width = heads * DH
    tokens = nblk * BLK
    nwin = GLOBAL + 3
    scale = 1.0 / DH**0.5

    kwin[:BLK] = left_ref[:, :width]
    vwin[:BLK] = left_ref[:, width:]
    kwin[BLK:BLK + tokens] = k_ref[...]
    vwin[BLK:BLK + tokens] = v_ref[...]
    kwin[BLK + tokens:] = right_ref[:, :width]
    vwin[BLK + tokens:] = right_ref[:, width:]
    ksel[:GLOBAL * BLK] = glob_ref[:, :width]
    vsel[:GLOBAL * BLK] = glob_ref[:, width:]
    acc_win[...] = jnp.zeros_like(acc_win)
    acc_glob[...] = jnp.zeros_like(acc_glob)
    acc_part[...] = jnp.zeros_like(acc_part)

    def step(b, carry):
        start = pl.multiple_of(b * BLK, BLK)
        rows = pl.ds(start, BLK)
        ksel[GLOBAL * BLK:nwin * BLK] = kwin[pl.ds(start, 3 * BLK)]
        vsel[GLOBAL * BLK:nwin * BLK] = vwin[pl.ds(start, 3 * BLK)]
        picks = []
        for r in range(RAND):
            pick = idx_ref[b * RAND + r]
            picks.append(pick)
            src = pl.ds(pl.multiple_of(pick * BLK, BLK), BLK)
            dst = slice((nwin + r) * BLK, (nwin + r + 1) * BLK)
            ksel[dst] = part_refs[r][src, :width]
            vsel[dst] = part_refs[r][src, width:]
        bias = bias_ref[b]
        hss = [slice(h * DH, (h + 1) * DH) for h in range(heads)]
        query = [q_ref[rows, hs] for hs in hss]
        dout = [do_ref[rows, hs] for hs in hss]
        scores = [dot(query[h], ksel[:, hss[h]], 1, 1) * scale + bias for h in range(heads)]
        dprobs = [dot(dout[h], vsel[:, hss[h]], 1, 1) for h in range(heads)]
        for h in range(heads):
            hs = hss[h]
            top = jnp.max(scores[h], axis=-1, keepdims=True)
            expo = jnp.exp(scores[h] - top)
            probs = expo * (1.0 / jnp.sum(expo, axis=-1, keepdims=True))
            probs_b = probs.astype(BF16)
            delta = jnp.sum(probs * dprobs[h], axis=-1, keepdims=True)
            dscores = (probs * (dprobs[h] - delta) * scale).astype(BF16)
            ctx_ref[rows, hs] = dot(probs_b, vsel[:, hs], 1, 0).astype(BF16)
            dq_ref[rows, hs] = dot(dscores, ksel[:, hs], 1, 0).astype(BF16)
            kterm = dot(query[h].T, dscores, 1, 0)
            vterm = dot(dout[h].T, probs_b, 1, 0)
            for base, term in ((h * DH, kterm), (width + h * DH, vterm)):
                at = slice(base, base + DH)
                for g in range(GLOBAL):
                    acc_glob[g, at] += term[:, g * BLK:(g + 1) * BLK]
                for w in range(3):
                    o = GLOBAL + w
                    acc_win[b + w, at] += term[:, o * BLK:(o + 1) * BLK]
                for r in range(RAND):
                    o = nwin + r
                    acc_part[r, picks[r], at] += term[:, o * BLK:(o + 1) * BLK]
        return carry

    lax.fori_loop(0, nblk, step, 0, unroll=4)
    gleft_ref[...] = acc_win[0].astype(BF16)
    gright_ref[...] = acc_win[nblk + 1].astype(BF16)
    own_ref[...] = acc_win[1:nblk + 1]
    gglob_ref[...] = acc_glob[...].astype(BF16)
    for r in range(RAND):
        gpart_refs[r][...] = acc_part[r].astype(BF16)


def finish_kernel(nblk, heads, first_ref, own_ref, low_ref, high_ref, glob_ref, *rest):
    part_refs = rest[:RAND]
    gk_ref, gv_ref = rest[RAND:]
    first = first_ref[0].astype(F32)
    width = heads * DH
    for b in range(nblk):
        rows = slice(b * BLK, (b + 1) * BLK)
        for c in range(2 * heads):
            at = slice(c * DH, (c + 1) * DH)
            total = own_ref[b, at]
            for r in range(RAND):
                total = total + part_refs[r][b, at].astype(F32)
            if b == 0:
                total = total + low_ref[at].astype(F32)
            if b == nblk - 1:
                total = total + high_ref[at].astype(F32)
            if b < GLOBAL:
                total = jnp.where(first > 0, glob_ref[b, at].astype(F32), total)
            out = gk_ref if c < heads else gv_ref
            h = c % heads
            out[rows, h * DH:(h + 1) * DH] = total.T.astype(BF16)


def exchange(x, axis):
    return lax.all_to_all(x, axis, 0, 0, tiled=True)


def spread(piece, count):
    return jnp.broadcast_to(piece[None], (count,) + piece.shape)


def total(pieces):
    return jnp.sum(pieces.astype(F32), axis=0).astype(BF16)


def tie(*values):
    return lax.optimization_barrier(values)


def shards(queries, keys, values, grad_out, rand_blocks):
    ny, nz = lax.axis_size("y"), lax.axis_size("z")
    n_seq = ny * nz
    myself = lax.axis_index("y") * nz + lax.axis_index("z")
    tokens, width = queries.shape
    nblk = tokens // BLK
    heads = width // DH
    nwin = GLOBAL + 3
    nkeys = (nwin + RAND) * BLK
    up = [(i, i + 1) for i in range(n_seq - 1)]
    down = [(j, i) for i, j in up]
    masks = [ny >> (r + 1) for r in range(RAND)]
    sds = jax.ShapeDtypeStruct
    params = pltpu.CompilerParams(vmem_limit_bytes=VMEM_LIMIT)

    def partner(x, r):
        return lax.ppermute(x, "y", [(i, i ^ masks[r]) for i in range(ny)])

    grows = GLOBAL * BLK
    glob = jnp.concatenate([keys[:grows], values[:grows]], axis=1)
    piece = exchange(glob.reshape(nz, grows // nz, 2 * width), "z")[0]
    kv = jnp.concatenate([keys, values], axis=1)
    left = lax.ppermute(kv[tokens - BLK:], SEQ_AXES, up)
    right = lax.ppermute(kv[:BLK], SEQ_AXES, down)
    far = partner(kv, 0)
    kv, piece = tie(kv, piece)
    fetched = [far] + [partner(kv, r) for r in range(1, RAND)]
    piece = exchange(spread(piece, ny), "y")[0]
    glob = exchange(spread(piece, nz), "z").reshape(grows, 2 * width)

    mine = lax.dynamic_slice_in_dim(rand_blocks, myself * nblk, nblk, 0)
    picks = (mine % nblk).reshape(-1)
    qblock = myself * nblk + jnp.arange(nblk, dtype=jnp.int32)
    window = qblock[:, None] + jnp.arange(-1, 2, dtype=jnp.int32)[None, :]
    live = jnp.concatenate(
        [jnp.ones((nblk, GLOBAL), bool), (window >= GLOBAL) & (window < nblk * n_seq), mine >= GLOBAL], axis=1)
    bias = jnp.repeat(jnp.where(live, 0.0, NEG).astype(F32), BLK, axis=1)[:, None, :]

    smem = pl.BlockSpec(memory_space=pltpu.SMEM)
    vmem = pl.BlockSpec(memory_space=pltpu.VMEM)
    outs = pl.pallas_call(
        lambda *refs: attention_kernel(nblk, heads, *refs),
        out_shape=[
            sds((tokens, width), BF16), sds((tokens, width), BF16),
            sds((nblk, 2 * width, BLK), F32), sds((2 * width, BLK), BF16), sds((2 * width, BLK), BF16),
            sds((GLOBAL, 2 * width, BLK), BF16),
        ] + [sds((nblk, 2 * width, BLK), BF16)] * RAND,
        in_specs=[smem] + [vmem] * (8 + RAND),
        out_specs=[vmem] * (6 + RAND),
        scratch_shapes=[
            pltpu.VMEM((tokens + 2 * BLK, width), BF16), pltpu.VMEM((tokens + 2 * BLK, width), BF16),
            pltpu.VMEM((nkeys, width), BF16), pltpu.VMEM((nkeys, width), BF16),
            pltpu.VMEM((nblk + 2, 2 * width, BLK), F32), pltpu.VMEM((GLOBAL, 2 * width, BLK), F32),
            pltpu.VMEM((RAND, nblk, 2 * width, BLK), F32),
        ],
        compiler_params=params,
        name="attention",
    )(picks, bias, queries, grad_out, keys, values, left, right, glob, *fetched)
    context, grad_q, own, gleft, gright, gglob = outs[:6]
    gparts = outs[6:]

    pieces = total(exchange(gglob.reshape(nz, -1, DH), "z"))
    far = partner(gparts[0], 0)
    far, gleft, gright, *gnear = tie(far, gleft, gright, *gparts[1:])
    back = [far] + [partner(g, r + 1) for r, g in enumerate(gnear)]
    high = lax.ppermute(gleft, SEQ_AXES, down)
    low = lax.ppermute(gright, SEQ_AXES, up)
    pieces = total(exchange(spread(pieces, ny), "y"))
    gsum = exchange(spread(pieces, nz), "z").reshape(GLOBAL, 2 * width, BLK)

    first = (myself == 0).astype(jnp.int32).reshape(1)
    grad_k, grad_v = pl.pallas_call(
        lambda *refs: finish_kernel(nblk, heads, *refs),
        out_shape=[sds((tokens, width), BF16), sds((tokens, width), BF16)],
        in_specs=[smem] + [vmem] * (4 + RAND),
        out_specs=[vmem] * 2,
        compiler_params=params,
        name="finish",
    )(first, own, low, high, gsum, *back)
    return context, grad_q, grad_k, grad_v


def solution(mesh):
    grid = Mesh(mesh.devices.reshape(8, 8, 8), ("y", "z", "head"))
    specs = (P(SEQ_AXES, "head"),) * 4
    return jax.shard_map(shards, mesh=grid, in_specs=specs + (P(),), out_specs=specs, check_vma=False)
```

```python
import jax
import jax.numpy as jnp
from jax import lax
from jax.experimental import pallas as pl
from jax.experimental.pallas import tpu as pltpu
from jax.sharding import Mesh, PartitionSpec as P

DH = 128
BLK = 128
GLOBAL = 2
RAND = 3
NEG = -1e30
F32 = jnp.float32
BF16 = jnp.bfloat16
SEQ_AXES = ("y", "z")
VMEM_LIMIT = 48 * 1024 * 1024


def dot(a, b, ca, cb):
    return lax.dot_general(a, b, (((ca,), (cb,)), ((), ())), preferred_element_type=F32)


def attention_kernel(nblk, heads, idx_ref, bias_ref, q_ref, do_ref, k_ref, v_ref, left_ref, right_ref,
                     glob_ref, *rest):
    part_refs = rest[:RAND]
    ctx_ref, dq_ref, own_ref, gleft_ref, gright_ref, gglob_ref = rest[RAND:RAND + 6]
    gpart_refs = rest[RAND + 6:2 * RAND + 6]
    kwin, vwin, ksel, vsel, acc_win, acc_glob, acc_part = rest[2 * RAND + 6:]
    width = heads * DH
    tokens = nblk * BLK
    nwin = GLOBAL + 3
    scale = 1.0 / DH**0.5

    kwin[:BLK] = left_ref[:, :width]
    vwin[:BLK] = left_ref[:, width:]
    kwin[BLK:BLK + tokens] = k_ref[...]
    vwin[BLK:BLK + tokens] = v_ref[...]
    kwin[BLK + tokens:] = right_ref[:, :width]
    vwin[BLK + tokens:] = right_ref[:, width:]
    ksel[:GLOBAL * BLK] = glob_ref[:, :width]
    vsel[:GLOBAL * BLK] = glob_ref[:, width:]
    acc_win[...] = jnp.zeros_like(acc_win)
    acc_glob[...] = jnp.zeros_like(acc_glob)
    acc_part[...] = jnp.zeros_like(acc_part)

    def step(b, carry):
        start = pl.multiple_of(b * BLK, BLK)
        rows = pl.ds(start, BLK)
        ksel[GLOBAL * BLK:nwin * BLK] = kwin[pl.ds(start, 3 * BLK)]
        vsel[GLOBAL * BLK:nwin * BLK] = vwin[pl.ds(start, 3 * BLK)]
        picks = []
        for r in range(RAND):
            pick = idx_ref[b * RAND + r]
            picks.append(pick)
            src = pl.ds(pl.multiple_of(pick * BLK, BLK), BLK)
            dst = slice((nwin + r) * BLK, (nwin + r + 1) * BLK)
            ksel[dst] = part_refs[r][src, :width]
            vsel[dst] = part_refs[r][src, width:]
        bias = bias_ref[b]
        hss = [slice(h * DH, (h + 1) * DH) for h in range(heads)]
        query = [q_ref[rows, hs] for hs in hss]
        dout = [do_ref[rows, hs] for hs in hss]
        scores = [dot(query[h], ksel[:, hss[h]], 1, 1) * scale + bias for h in range(heads)]
        dprobs = [dot(dout[h], vsel[:, hss[h]], 1, 1) for h in range(heads)]
        for h in range(heads):
            hs = hss[h]
            top = jnp.max(scores[h], axis=-1, keepdims=True)
            expo = jnp.exp(scores[h] - top)
            probs = expo * (1.0 / jnp.sum(expo, axis=-1, keepdims=True))
            probs_b = probs.astype(BF16)
            delta = jnp.sum(probs * dprobs[h], axis=-1, keepdims=True)
            dscores = (probs * (dprobs[h] - delta) * scale).astype(BF16)
            ctx_ref[rows, hs] = dot(probs_b, vsel[:, hs], 1, 0).astype(BF16)
            dq_ref[rows, hs] = dot(dscores, ksel[:, hs], 1, 0).astype(BF16)
            kterm = dot(query[h].T, dscores, 1, 0)
            vterm = dot(dout[h].T, probs_b, 1, 0)
            for base, term in ((h * DH, kterm), (width + h * DH, vterm)):
                at = slice(base, base + DH)
                for g in range(GLOBAL):
                    acc_glob[g, at] += term[:, g * BLK:(g + 1) * BLK]
                for w in range(3):
                    o = GLOBAL + w
                    acc_win[b + w, at] += term[:, o * BLK:(o + 1) * BLK]
                for r in range(RAND):
                    o = nwin + r
                    acc_part[r, picks[r], at] += term[:, o * BLK:(o + 1) * BLK]
        return carry

    lax.fori_loop(0, nblk, step, 0, unroll=4)
    gleft_ref[...] = acc_win[0].astype(BF16)
    gright_ref[...] = acc_win[nblk + 1].astype(BF16)
    own_ref[...] = acc_win[1:nblk + 1]
    gglob_ref[...] = acc_glob[...].astype(BF16)
    for r in range(RAND):
        gpart_refs[r][...] = acc_part[r].astype(BF16)


def finish_kernel(nblk, heads, first_ref, own_ref, low_ref, high_ref, glob_ref, *rest):
    part_refs = rest[:RAND]
    gk_ref, gv_ref = rest[RAND:]
    first = first_ref[0].astype(F32)
    width = heads * DH
    for b in range(nblk):
        rows = slice(b * BLK, (b + 1) * BLK)
        for c in range(2 * heads):
            at = slice(c * DH, (c + 1) * DH)
            total = own_ref[b, at]
            for r in range(RAND):
                total = total + part_refs[r][b, at].astype(F32)
            if b == 0:
                total = total + low_ref[at].astype(F32)
            if b == nblk - 1:
                total = total + high_ref[at].astype(F32)
            if b < GLOBAL:
                total = jnp.where(first > 0, glob_ref[b, at].astype(F32), total)
            out = gk_ref if c < heads else gv_ref
            h = c % heads
            out[rows, h * DH:(h + 1) * DH] = total.T.astype(BF16)


def exchange(x, axis):
    return lax.all_to_all(x, axis, 0, 0, tiled=True)


def spread(piece, count):
    return jnp.broadcast_to(piece[None], (count,) + piece.shape)


def total(pieces):
    return jnp.sum(pieces.astype(F32), axis=0).astype(BF16)


def tie(*values):
    return lax.optimization_barrier(values)


def shards(queries, keys, values, grad_out, rand_blocks):
    ny, nz = lax.axis_size("y"), lax.axis_size("z")
    n_seq = ny * nz
    myself = lax.axis_index("y") * nz + lax.axis_index("z")
    tokens, width = queries.shape
    nblk = tokens // BLK
    heads = width // DH
    nwin = GLOBAL + 3
    nkeys = (nwin + RAND) * BLK
    up = [(i, i + 1) for i in range(n_seq - 1)]
    down = [(j, i) for i, j in up]
    masks = [ny >> (r + 1) for r in range(RAND)]
    sds = jax.ShapeDtypeStruct
    params = pltpu.CompilerParams(vmem_limit_bytes=VMEM_LIMIT)

    def partner(x, r):
        return lax.ppermute(x, "y", [(i, i ^ masks[r]) for i in range(ny)])

    grows = GLOBAL * BLK
    glob = jnp.concatenate([keys[:grows], values[:grows]], axis=1)
    piece = exchange(glob.reshape(nz, grows // nz, 2 * width), "z")[0]
    kv = jnp.concatenate([keys, values], axis=1)
    left = lax.ppermute(kv[tokens - BLK:], SEQ_AXES, up)
    right = lax.ppermute(kv[:BLK], SEQ_AXES, down)
    far = partner(kv, 0)
    kv, piece = tie(kv, piece)
    one = partner(kv, 2)
    kv, far = tie(kv, far)
    fetched = [far, partner(kv, 1), one]
    piece = exchange(spread(piece, ny), "y")[0]
    glob = exchange(spread(piece, nz), "z").reshape(grows, 2 * width)

    mine = lax.dynamic_slice_in_dim(rand_blocks, myself * nblk, nblk, 0)
    picks = (mine % nblk).reshape(-1)
    qblock = myself * nblk + jnp.arange(nblk, dtype=jnp.int32)
    window = qblock[:, None] + jnp.arange(-1, 2, dtype=jnp.int32)[None, :]
    live = jnp.concatenate(
        [jnp.ones((nblk, GLOBAL), bool), (window >= GLOBAL) & (window < nblk * n_seq), mine >= GLOBAL], axis=1)
    bias = jnp.repeat(jnp.where(live, 0.0, NEG).astype(F32), BLK, axis=1)[:, None, :]

    smem = pl.BlockSpec(memory_space=pltpu.SMEM)
    vmem = pl.BlockSpec(memory_space=pltpu.VMEM)
    outs = pl.pallas_call(
        lambda *refs: attention_kernel(nblk, heads, *refs),
        out_shape=[
            sds((tokens, width), BF16), sds((tokens, width), BF16),
            sds((nblk, 2 * width, BLK), F32), sds((2 * width, BLK), BF16), sds((2 * width, BLK), BF16),
            sds((GLOBAL, 2 * width, BLK), BF16),
        ] + [sds((nblk, 2 * width, BLK), BF16)] * RAND,
        in_specs=[smem] + [vmem] * (8 + RAND),
        out_specs=[vmem] * (6 + RAND),
        scratch_shapes=[
            pltpu.VMEM((tokens + 2 * BLK, width), BF16), pltpu.VMEM((tokens + 2 * BLK, width), BF16),
            pltpu.VMEM((nkeys, width), BF16), pltpu.VMEM((nkeys, width), BF16),
            pltpu.VMEM((nblk + 2, 2 * width, BLK), F32), pltpu.VMEM((GLOBAL, 2 * width, BLK), F32),
            pltpu.VMEM((RAND, nblk, 2 * width, BLK), F32),
        ],
        compiler_params=params,
        name="attention",
    )(picks, bias, queries, grad_out, keys, values, left, right, glob, *fetched)
    context, grad_q, own, gleft, gright, gglob = outs[:6]
    gparts = outs[6:]

    pieces = total(exchange(gglob.reshape(nz, -1, DH), "z"))
    far = partner(gparts[0], 0)
    pieces, gtwo = tie(pieces, gparts[1])
    back = [far, partner(gtwo, 1), None]
    back[0], gleft, gright, gone = tie(far, gleft, gright, gparts[2])
    back[2] = partner(gone, 2)
    high = lax.ppermute(gleft, SEQ_AXES, down)
    low = lax.ppermute(gright, SEQ_AXES, up)
    pieces = total(exchange(spread(pieces, ny), "y"))
    gsum = exchange(spread(pieces, nz), "z").reshape(GLOBAL, 2 * width, BLK)

    first = (myself == 0).astype(jnp.int32).reshape(1)
    grad_k, grad_v = pl.pallas_call(
        lambda *refs: finish_kernel(nblk, heads, *refs),
        out_shape=[sds((tokens, width), BF16), sds((tokens, width), BF16)],
        in_specs=[smem] + [vmem] * (4 + RAND),
        out_specs=[vmem] * 2,
        compiler_params=params,
        name="finish",
    )(first, own, low, high, gsum, *back)
    return context, grad_q, grad_k, grad_v


def solution(mesh):
    grid = Mesh(mesh.devices.reshape(8, 8, 8), ("y", "z", "head"))
    specs = (P(SEQ_AXES, "head"),) * 4
    return jax.shard_map(shards, mesh=grid, in_specs=specs + (P(),), out_specs=specs, check_vma=False)
```

```python
import jax
import jax.numpy as jnp
from jax import lax
from jax.experimental import pallas as pl
from jax.experimental.pallas import tpu as pltpu
from jax.sharding import Mesh, PartitionSpec as P

DH = 128
BLK = 128
GLOBAL = 2
RAND = 3
NEG = -1e30
F32 = jnp.float32
BF16 = jnp.bfloat16
SEQ_AXES = ("y", "z")
VMEM_LIMIT = 48 * 1024 * 1024


def dot(a, b, ca, cb):
    return lax.dot_general(a, b, (((ca,), (cb,)), ((), ())), preferred_element_type=F32)


def attention_kernel(nblk, heads, idx_ref, bias_ref, q_ref, do_ref, k_ref, v_ref, left_ref, right_ref,
                     glob_ref, *rest):
    part_refs = rest[:RAND]
    ctx_ref, dq_ref, own_ref, gleft_ref, gright_ref, gglob_ref = rest[RAND:RAND + 6]
    gpart_refs = rest[RAND + 6:2 * RAND + 6]
    kwin, vwin, ksel, vsel, acc_win, acc_glob, acc_part = rest[2 * RAND + 6:]
    width = heads * DH
    tokens = nblk * BLK
    nwin = GLOBAL + 3
    scale = 1.0 / DH**0.5

    kwin[:BLK] = left_ref[:, :width]
    vwin[:BLK] = left_ref[:, width:]
    kwin[BLK:BLK + tokens] = k_ref[...]
    vwin[BLK:BLK + tokens] = v_ref[...]
    kwin[BLK + tokens:] = right_ref[:, :width]
    vwin[BLK + tokens:] = right_ref[:, width:]
    ksel[:GLOBAL * BLK] = glob_ref[:GLOBAL * BLK]
    vsel[:GLOBAL * BLK] = glob_ref[GLOBAL * BLK:]
    acc_win[...] = jnp.zeros_like(acc_win)
    acc_glob[...] = jnp.zeros_like(acc_glob)
    acc_part[...] = jnp.zeros_like(acc_part)

    def step(b, carry):
        start = pl.multiple_of(b * BLK, BLK)
        rows = pl.ds(start, BLK)
        ksel[GLOBAL * BLK:nwin * BLK] = kwin[pl.ds(start, 3 * BLK)]
        vsel[GLOBAL * BLK:nwin * BLK] = vwin[pl.ds(start, 3 * BLK)]
        picks = []
        for r in range(RAND):
            pick = idx_ref[b * RAND + r]
            picks.append(pick)
            src = pl.ds(pl.multiple_of(pick * BLK, BLK), BLK)
            dst = slice((nwin + r) * BLK, (nwin + r + 1) * BLK)
            ksel[dst] = part_refs[r][src, :width]
            vsel[dst] = part_refs[r][src, width:]
        bias = bias_ref[b]
        hss = [slice(h * DH, (h + 1) * DH) for h in range(heads)]
        query = [q_ref[rows, hs] for hs in hss]
        dout = [do_ref[rows, hs] for hs in hss]
        scores = [dot(query[h], ksel[:, hss[h]], 1, 1) * scale + bias for h in range(heads)]
        dprobs = [dot(dout[h], vsel[:, hss[h]], 1, 1) for h in range(heads)]
        for h in range(heads):
            hs = hss[h]
            top = jnp.max(scores[h], axis=-1, keepdims=True)
            expo = jnp.exp(scores[h] - top)
            probs = expo * (1.0 / jnp.sum(expo, axis=-1, keepdims=True))
            probs_b = probs.astype(BF16)
            delta = jnp.sum(probs * dprobs[h], axis=-1, keepdims=True)
            dscores = (probs * (dprobs[h] - delta) * scale).astype(BF16)
            ctx_ref[rows, hs] = dot(probs_b, vsel[:, hs], 1, 0).astype(BF16)
            dq_ref[rows, hs] = dot(dscores, ksel[:, hs], 1, 0).astype(BF16)
            kterm = dot(query[h].T, dscores, 1, 0)
            vterm = dot(dout[h].T, probs_b, 1, 0)
            for base, term in ((h * DH, kterm), (width + h * DH, vterm)):
                at = slice(base, base + DH)
                for g in range(GLOBAL):
                    acc_glob[g, at] += term[:, g * BLK:(g + 1) * BLK]
                for w in range(3):
                    o = GLOBAL + w
                    acc_win[b + w, at] += term[:, o * BLK:(o + 1) * BLK]
                for r in range(RAND):
                    o = nwin + r
                    acc_part[r, picks[r], at] += term[:, o * BLK:(o + 1) * BLK]
        return carry

    lax.fori_loop(0, nblk, step, 0, unroll=4)
    gleft_ref[...] = acc_win[0].astype(BF16)
    gright_ref[...] = acc_win[nblk + 1].astype(BF16)
    own_ref[...] = acc_win[1:nblk + 1]
    gglob_ref[...] = acc_glob[...].astype(BF16)
    for r in range(RAND):
        gpart_refs[r][...] = acc_part[r].astype(BF16)


def finish_kernel(nblk, heads, first_ref, own_ref, low_ref, high_ref, glob_ref, *rest):
    part_refs = rest[:RAND]
    gk_ref, gv_ref = rest[RAND:]
    first = first_ref[0].astype(F32)
    width = heads * DH
    for b in range(nblk):
        rows = slice(b * BLK, (b + 1) * BLK)
        for c in range(2 * heads):
            at = slice(c * DH, (c + 1) * DH)
            total = own_ref[b, at]
            for r in range(RAND):
                total = total + part_refs[r][b, at].astype(F32)
            if b == 0:
                total = total + low_ref[at].astype(F32)
            if b == nblk - 1:
                total = total + high_ref[at].astype(F32)
            if b < GLOBAL:
                total = jnp.where(first > 0, glob_ref[b, at].astype(F32), total)
            out = gk_ref if c < heads else gv_ref
            h = c % heads
            out[rows, h * DH:(h + 1) * DH] = total.T.astype(BF16)


def exchange(x, axis):
    return lax.all_to_all(x, axis, 0, 0, tiled=True)


def spread(piece, count):
    return jnp.broadcast_to(piece[None], (count,) + piece.shape)


def total(pieces):
    return jnp.sum(pieces.astype(F32), axis=0).astype(BF16)


def tie(*values):
    return lax.optimization_barrier(values)


def shards(queries, keys, values, grad_out, rand_blocks):
    ny, nz = lax.axis_size("y"), lax.axis_size("z")
    n_seq = ny * nz
    myself = lax.axis_index("y") * nz + lax.axis_index("z")
    tokens, width = queries.shape
    nblk = tokens // BLK
    heads = width // DH
    nwin = GLOBAL + 3
    nkeys = (nwin + RAND) * BLK
    up = [(i, i + 1) for i in range(n_seq - 1)]
    down = [(j, i) for i, j in up]
    masks = [ny >> (r + 1) for r in range(RAND)]
    sds = jax.ShapeDtypeStruct
    params = pltpu.CompilerParams(vmem_limit_bytes=VMEM_LIMIT)

    def partner(x, r):
        return lax.ppermute(x, "y", [(i, i ^ masks[r]) for i in range(ny)])

    grows = GLOBAL * BLK
    glob = jnp.concatenate([keys[:grows], values[:grows]], axis=0)
    piece = exchange(glob.reshape(nz, 2 * grows // nz, width), "z")[0]
    kv = jnp.concatenate([keys, values], axis=1)
    left = lax.ppermute(kv[tokens - BLK:], SEQ_AXES, up)
    right = lax.ppermute(kv[:BLK], SEQ_AXES, down)
    far = partner(kv, 0)
    kv, piece = tie(kv, piece)
    one = partner(kv, 2)
    kv, far = tie(kv, far)
    fetched = [far, partner(kv, 1), one]
    piece = exchange(spread(piece, ny), "y")[0]
    glob = exchange(spread(piece, nz), "z").reshape(2 * grows, width)

    mine = lax.dynamic_slice_in_dim(rand_blocks, myself * nblk, nblk, 0)
    picks = (mine % nblk).reshape(-1)
    qblock = myself * nblk + jnp.arange(nblk, dtype=jnp.int32)
    window = qblock[:, None] + jnp.arange(-1, 2, dtype=jnp.int32)[None, :]
    live = jnp.concatenate(
        [jnp.ones((nblk, GLOBAL), bool), (window >= GLOBAL) & (window < nblk * n_seq), mine >= GLOBAL], axis=1)
    bias = jnp.repeat(jnp.where(live, 0.0, NEG).astype(F32), BLK, axis=1)[:, None, :]

    smem = pl.BlockSpec(memory_space=pltpu.SMEM)
    vmem = pl.BlockSpec(memory_space=pltpu.VMEM)
    outs = pl.pallas_call(
        lambda *refs: attention_kernel(nblk, heads, *refs),
        out_shape=[
            sds((tokens, width), BF16), sds((tokens, width), BF16),
            sds((nblk, 2 * width, BLK), F32), sds((2 * width, BLK), BF16), sds((2 * width, BLK), BF16),
            sds((GLOBAL, 2 * width, BLK), BF16),
        ] + [sds((nblk, 2 * width, BLK), BF16)] * RAND,
        in_specs=[smem] + [vmem] * (8 + RAND),
        out_specs=[vmem] * (6 + RAND),
        scratch_shapes=[
            pltpu.VMEM((tokens + 2 * BLK, width), BF16), pltpu.VMEM((tokens + 2 * BLK, width), BF16),
            pltpu.VMEM((nkeys, width), BF16), pltpu.VMEM((nkeys, width), BF16),
            pltpu.VMEM((nblk + 2, 2 * width, BLK), F32), pltpu.VMEM((GLOBAL, 2 * width, BLK), F32),
            pltpu.VMEM((RAND, nblk, 2 * width, BLK), F32),
        ],
        compiler_params=params,
        name="attention",
    )(picks, bias, queries, grad_out, keys, values, left, right, glob, *fetched)
    context, grad_q, own, gleft, gright, gglob = outs[:6]
    gparts = outs[6:]

    pieces = total(exchange(gglob.reshape(nz, -1, DH), "z"))
    far = partner(gparts[0], 0)
    pieces, gtwo = tie(pieces, gparts[1])
    back = [far, partner(gtwo, 1), None]
    back[0], gleft, gright, gone = tie(far, gleft, gright, gparts[2])
    back[2] = partner(gone, 2)
    high = lax.ppermute(gleft, SEQ_AXES, down)
    low = lax.ppermute(gright, SEQ_AXES, up)
    pieces = total(exchange(spread(pieces, ny), "y"))
    gsum = exchange(spread(pieces, nz), "z").reshape(GLOBAL, 2 * width, BLK)

    first = (myself == 0).astype(jnp.int32).reshape(1)
    grad_k, grad_v = pl.pallas_call(
        lambda *refs: finish_kernel(nblk, heads, *refs),
        out_shape=[sds((tokens, width), BF16), sds((tokens, width), BF16)],
        in_specs=[smem] + [vmem] * (4 + RAND),
        out_specs=[vmem] * 2,
        compiler_params=params,
        name="finish",
    )(first, own, low, high, gsum, *back)
    return context, grad_q, grad_k, grad_v


def solution(mesh):
    grid = Mesh(mesh.devices.reshape(8, 8, 8), ("y", "z", "head"))
    specs = (P(SEQ_AXES, "head"),) * 4
    return jax.shard_map(shards, mesh=grid, in_specs=specs + (P(),), out_specs=specs, check_vma=False)
```
